32 devices in a mesh: grp: 4 (over y, core), scen: 8 (over z, x).
Axes of the slice: x: 2, y: 2, z: 4, core: 2. Of those that a mesh axis runs over, the one named last changes fastest.
Arguments:
- linv: bfloat16 [64, 2048, 2048], P(('grp', 'scen'))
- link: bfloat16 [64, 2048, 512], P(('grp', 'scen')), may hold values from -0.125 to 0.125
- residual_rows: bfloat16 [64, 2048], P(('grp', 'scen')), may hold values from -24 to 24
- active: int32 [64], P(('grp', 'scen')), may hold values from 512 to 2048
- owner: int32 [64], P(('grp', 'scen')), may hold values from 0 to 63, each once
- weights: float32 [64], replicated, may hold values from 0.01 to 0.1
- first_diag: float32 [512], replicated, may hold values from 1 to 10
- first_rhs: float32 [512], replicated, may hold values from -24 to 24
Outputs:
- step_first: float32 [512], replicated
- scenario_newton_step: float32 [64, 2048], P(('grp', 'scen'))
The draws below stay inside these ranges and needn't reach their ends.
All inputs are finite; a program needn't handle non-finite values.
Results may differ from the reference program's by a relative error of at most 0.0075.
Values sent between devices are 32-bit elements; how exact they have to be, the bound alone decides.
A program may use at most 128 MiB of HBM per device.

```python
import math
import jax
import jax.numpy as jnp
from jax import lax

P_SIZE = 512
M = 2048
ITERS = 2
SCEN = 64


def draw_linv(key, part):
    keys = jax.random.split(jax.random.fold_in(key, 11), SCEN)

    def single(inner):
        first, second = jax.random.split(inner, 2)
        lower = jnp.tril(jax.random.normal(first, (M, M), jnp.float32) * (0.5 / jnp.sqrt(M * 1.0)), -1)
        diagonal = jnp.exp(jax.random.uniform(second, (M,), jnp.float32, jnp.log(0.5), jnp.log(2.0)))
        matrix = lower + jnp.eye(M, dtype=jnp.float32) * diagonal[None, :]
        return matrix.astype(jnp.bfloat16)
    return lax.map(single, keys)


def touch_ends(entries, key, least, high):
    longest = entries.shape.index(max(entries.shape))
    spots = []
    for shift in (0, 1):
        where = [jax.random.randint(jax.random.fold_in(key, axis), (), 0, length) for axis, length in enumerate(entries.shape)]
        where[longest] = (where[longest] + shift) % entries.shape[longest]
        spots.append(tuple(where))
    return entries.at[spots[0]].set(least).at[spots[1]].set(high)


def levels(own_key, dims, cuts, least, high):
    def one(position, parts):
        steps = jax.random.uniform(jax.random.fold_in(jax.random.fold_in(own_key, 6), position), (parts,), jnp.float32, least / len(cuts), high / len(cuts))
        return jnp.repeat(jnp.exp(steps), dims[position] // parts).reshape((-1,) + (1,) * (len(dims) - position - 1))

    gain = one(*cuts[0])
    for cut in cuts[1:]:
        gain = gain * one(*cut)
    return gain


def normal_values(stream_key, dims, spread, reach, shards=(), kind=jnp.bfloat16):
    level = levels(stream_key, dims, shards, -0.22, 0.18) if shards else 1.0
    array = jax.random.normal(stream_key, dims, jnp.float32) * spread * level
    return jnp.minimum(jnp.maximum(array, -reach), reach).astype(kind)


def setup_inputs(seed: int = 0) -> dict:
    streams_of = jax.random.split(jax.random.key(seed), 9)
    linv = draw_linv(jax.random.fold_in(streams_of[8], 71), 0)
    link = normal_values(streams_of[1], (SCEN, M, P_SIZE), M ** -0.5, 0.125, ((0, 32),))
    residual_rows = normal_values(streams_of[2], (SCEN, M), 4.0, 24.0, ((0, 32),))
    active = touch_ends(jax.random.randint(streams_of[3], (SCEN,), M // 4, M + 1), jax.random.fold_in(streams_of[3], 1), M // 4, M).astype(jnp.int32)
    owner = jax.random.permutation(streams_of[4], SCEN).astype(jnp.int32)
    weights = jnp.clip(jnp.exp(jax.random.uniform(streams_of[5], (SCEN,), jnp.float32, math.log(0.01), math.log(0.1))), 0.01, 0.1)
    first_diag = jnp.clip(jnp.exp(jax.random.uniform(streams_of[6], (P_SIZE,), jnp.float32, math.log(1.0), math.log(10.0))), 1.0, 10.0)
    first_rhs = normal_values(streams_of[7], (P_SIZE,), 4.0, 24.0, (), jnp.float32)
    return {"linv": linv, "link": link, "residual_rows": residual_rows, "active": active, "owner": owner, "weights": weights, "first_diag": first_diag, "first_rhs": first_rhs}


def reference(linv, link, residual_rows, active, owner, weights, first_diag, first_rhs):
    probs = weights[owner]
    rows = jnp.arange(M, dtype=jnp.int32)

    def prepare(matrix, columns, right, count):
        keep = rows < count
        masked = jnp.where(keep[:, None], columns, jnp.zeros_like(columns))
        solved = jnp.dot(matrix, masked, preferred_element_type=jnp.float32).astype(jnp.bfloat16)
        lifted = jnp.dot(matrix, right, preferred_element_type=jnp.float32).astype(jnp.bfloat16)
        return solved, lifted

    def accumulate(carry, entry_element):
        matrix, columns, right, count, weight = entry_element
        solved, lifted = prepare(matrix, columns, right, count)
        gram = jnp.dot(solved.T, solved, preferred_element_type=jnp.float32)
        cross = jnp.dot(lifted, solved, preferred_element_type=jnp.float32)
        return (carry[0] + weight * gram, carry[1] + weight * cross), None

    start = (jnp.zeros((P_SIZE, P_SIZE), jnp.float32), jnp.zeros((P_SIZE,), jnp.float32))
    (schur_sum, cross_sum), unused = lax.scan(accumulate, start, (linv, link, residual_rows, active, probs))
    schur = jnp.diag(first_diag) + schur_sum
    vector = first_rhs - cross_sum
    iterate = jnp.zeros_like(vector)
    remain = vector
    direction = vector
    norm_now = jnp.sum(remain * remain)
    for step in range(ITERS):
        image = jnp.dot(schur, direction, precision=lax.Precision.HIGHEST)
        alpha = norm_now / jnp.sum(direction * image)
        iterate = iterate + alpha * direction
        remain = remain - alpha * image
        norm_next = jnp.sum(remain * remain)
        direction = remain + (norm_next / norm_now) * direction
        norm_now = norm_next
    step_first = iterate
    step_bf = step_first.astype(jnp.bfloat16)

    def back_solve(entry_element):
        matrix, columns, right, count = entry_element
        solved, lifted = prepare(matrix, columns, right, count)
        residue = lifted.astype(jnp.float32) - jnp.dot(solved, step_bf, preferred_element_type=jnp.float32)
        return jnp.dot(residue.astype(jnp.bfloat16), matrix, preferred_element_type=jnp.float32)

    scenario_newton_step = lax.map(back_solve, (linv, link, residual_rows, active))
    return step_first, scenario_newton_step
```

```python
import functools
import math

import jax
import jax.numpy as jnp
from jax import lax
from jax.experimental import pallas as pl
from jax.experimental.pallas import tpu as pltpu
from jax.sharding import PartitionSpec as P

MESH = pl.DeviceIdType.MESH
NT = (((1,), (1,)), ((), ()))
BLOCK = 256
PAD = 16
LANES = 128
ROUNDS = 3
STAGES = (("grp",), ("scen",))


def member(axes, sizes, shift):
    me = 0
    for axis in axes:
        me = me * sizes[axis] + lax.axis_index(axis)
    other = lax.rem(me + shift, math.prod(sizes[axis] for axis in axes))
    place = {}
    for axis in reversed(axes):
        place[axis] = lax.rem(other, sizes[axis])
        other = lax.div(other, sizes[axis])
    return me, place


def split(row):
    high = row.astype(jnp.bfloat16).astype(jnp.float32)
    return high, row - high


def stack(rows):
    width = rows[0].shape[1]
    numbers = lax.broadcasted_iota(jnp.int32, (PAD, width), 0)
    out = jnp.zeros((PAD, width), jnp.float32)
    for number, row in enumerate(rows):
        out = jnp.where(numbers == number, row, out)
    return out.astype(jnp.bfloat16)


def to_tile(row, tile_rows):
    pieces = [row[:, at : at + LANES] for at in range(0, row.shape[1], LANES)]
    if len(pieces) < tile_rows:
        pieces.append(jnp.zeros((tile_rows - len(pieces), LANES), jnp.float32))
    return jnp.concatenate(pieces, axis=0)


def to_row(tile, width):
    return jnp.concatenate([tile[n : n + 1, :] for n in range(width // LANES)], axis=1)


def kernel(
    sizes,
    active_ref,
    owner_ref,
    weights_ref,
    residual_ref,
    diag_ref,
    rhs_ref,
    linv_hbm,
    link_hbm,
    step_ref,
    newton_ref,
    linv,
    link,
    lhs,
    solved,
    gram,
    back,
    *rest,
):
    count, rows, width = link.shape
    blocks = rows // BLOCK
    bufs = rest[: len(STAGES)]
    linv_sem, link_sem = rest[len(STAGES) : len(STAGES) + 2]
    send_sems = rest[len(STAGES) + 2 : 2 * len(STAGES) + 2]
    recv_sems = rest[2 * len(STAGES) + 2 :]
    tile_rows = bufs[0].shape[2]

    barrier = pltpu.get_barrier_semaphore()
    partners = 0
    for axes in STAGES:
        for shift in range(1, math.prod(sizes[axis] for axis in axes)):
            pl.semaphore_signal(
                barrier, inc=1, device_id=member(axes, sizes, shift)[1], device_id_type=MESH
            )
            partners += 1

    def linv_copy(s, i):
        part = (s, pl.ds(i * BLOCK, BLOCK), pl.ds(0, (i + 1) * BLOCK))
        return pltpu.make_async_copy(linv_hbm.at[part], linv.at[part], linv_sem.at[s, i])

    def link_copy(s, i):
        part = (s, pl.ds(i * BLOCK, BLOCK))
        return pltpu.make_async_copy(link_hbm.at[part], link.at[part], link_sem.at[s, i])

    for s in range(count):
        for i in range(blocks):
            link_copy(s, i).start()
            linv_copy(s, i).start()

    right = residual_ref[...].astype(jnp.float32)
    for s in range(count):
        lhs[s, width:, :] = stack([right[s : s + 1, :]])

    def turn(s, i):
        link_copy(s, i).wait()
        columns = link[s, i * BLOCK : (i + 1) * BLOCK, :].astype(jnp.float32)
        numbers = i * BLOCK + lax.broadcasted_iota(jnp.int32, (BLOCK, width), 0)
        masked = jnp.where(numbers < active_ref[s], columns, 0.0).astype(jnp.bfloat16)
        lhs[s, :width, i * BLOCK : (i + 1) * BLOCK] = masked.T

    def prepare(s, cross):
        turn(s, 0)
        for i in range(blocks):
            linv_copy(s, i).wait()
            if i + 1 < blocks:
                turn(s, i + 1)
            deep = (i + 1) * BLOCK
            out = lax.dot_general(
                lhs[s, :, :deep],
                linv[s, i * BLOCK : deep, :deep],
                NT,
                preferred_element_type=jnp.float32,
            )
            solved[s, :, i * BLOCK : deep] = out.astype(jnp.bfloat16)
        part = lax.dot_general(
            solved[s, width:, :], solved[s, :width, :], NT, preferred_element_type=jnp.float32
        )
        return cross + weights_ref[owner_ref[s]] * part[0:1, :]

    cross = lax.fori_loop(0, count, prepare, jnp.zeros((1, width), jnp.float32))
    pl.semaphore_wait(barrier, partners)

    def total(turn_number, tile, beside):
        for stage, axes in enumerate(STAGES):
            buf = bufs[stage]
            n = buf.shape[1]
            me = member(axes, sizes, 0)[0]
            buf[turn_number, me] = tile
            copies = []
            for shift in range(1, n):
                copies.append(
                    pltpu.make_async_remote_copy(
                        src_ref=buf.at[turn_number, me],
                        dst_ref=buf.at[turn_number, me],
                        send_sem=send_sems[stage].at[turn_number, shift],
                        recv_sem=recv_sems[stage].at[turn_number, shift],
                        device_id=member(axes, sizes, shift)[1],
                        device_id_type=MESH,
                    )
                )
                copies[-1].start()
            for s in range(count):
                if s * len(STAGES) // count == stage:
                    beside(s)
            for copy in copies:
                copy.wait()
            tile = buf[turn_number, 0]
            for number in range(1, n):
                tile = tile + buf[turn_number, number]
        return tile

    def add_gram(s):
        part = lax.dot_general(
            solved[s, :width, :], solved[s, :width, :], NT, preferred_element_type=jnp.float32
        )
        part = weights_ref[owner_ref[s]] * part
        gram[...] = part if s == 0 else gram[...] + part

    def times_gram(row):
        spread = jnp.broadcast_to(row, (8, width))
        out = jnp.dot(
            spread, gram[...], precision=lax.Precision.HIGHEST, preferred_element_type=jnp.float32
        )
        return out[0:1, :]

    def dots(left, other):
        return jnp.sum(left * other, axis=1, keepdims=True)

    diag = diag_ref[...]
    vector = rhs_ref[...] - to_row(total(0, to_tile(cross, tile_rows), add_gram), width)
    norm_first = dots(vector, vector)
    summed = total(1, to_tile(times_gram(vector), tile_rows), lambda s: None)
    image = diag * vector + to_row(summed, width)
    alpha = norm_first / dots(vector, image)
    iterate = alpha * vector
    remain = vector - alpha * image
    norm_next = dots(remain, remain)
    direction = remain + (norm_next / norm_first) * vector
    local = dots(direction, times_gram(direction))
    both = stack([*split(iterate), *split(direction)])

    def back_solve(s):
        taken = jnp.dot(both, solved[s, :width, :], preferred_element_type=jnp.float32)
        lifted = solved[s, width:, :].astype(jnp.float32)[0:1, :]
        residue = lifted - (taken[0:1, :] + taken[1:2, :])
        slope = taken[2:3, :] + taken[3:4, :]
        sides = stack([*split(residue), *split(slope)])
        for j in range(blocks):
            back[s, :, j * BLOCK : (j + 1) * BLOCK] = jnp.dot(
                sides[:, j * BLOCK :],
                linv[s, j * BLOCK :, j * BLOCK : (j + 1) * BLOCK],
                preferred_element_type=jnp.float32,
            )

    curved = total(2, jnp.broadcast_to(local, (tile_rows, LANES)), back_solve)[0:1, 0:1]
    alpha = norm_next / (dots(direction, diag * direction) + curved)
    step_ref[...] = iterate + alpha * direction
    for s in range(count):
        newton_ref[s : s + 1, :] = (back[s, 0:1, :] + back[s, 1:2, :]) - alpha * (
            back[s, 2:3, :] + back[s, 3:4, :]
        )


def body(sizes, linv, link, residual_rows, active, owner, weights, first_diag, first_rhs):
    count, rows, width = link.shape
    blocks = rows // BLOCK
    tile_rows = -(-width // (8 * LANES)) * 8
    members = [math.prod(sizes[axis] for axis in axes) for axes in STAGES]
    smem = pl.BlockSpec(memory_space=pltpu.SMEM)
    vmem = pl.BlockSpec(memory_space=pltpu.VMEM)
    hbm = pl.BlockSpec(memory_space=pl.ANY)
    step, newton = pl.pallas_call(
        functools.partial(kernel, sizes),
        out_shape=(
            jax.ShapeDtypeStruct((1, width), jnp.float32),
            jax.ShapeDtypeStruct((count, rows), jnp.float32),
        ),
        in_specs=[smem, smem, smem, vmem, vmem, vmem, hbm, hbm],
        out_specs=(vmem, vmem),
        scratch_shapes=[
            pltpu.VMEM((count, rows, rows), jnp.bfloat16),
            pltpu.VMEM((count, rows, width), jnp.bfloat16),
            pltpu.VMEM((count, width + PAD, rows), jnp.bfloat16),
            pltpu.VMEM((count, width + PAD, rows), jnp.bfloat16),
            pltpu.VMEM((width, width), jnp.float32),
            pltpu.VMEM((count, PAD, rows), jnp.float32),
            *[pltpu.VMEM((ROUNDS, n, tile_rows, LANES), jnp.float32) for n in members],
            pltpu.SemaphoreType.DMA((count, blocks)),
            pltpu.SemaphoreType.DMA((count, blocks)),
            *[pltpu.SemaphoreType.DMA((ROUNDS, n)) for n in members],
            *[pltpu.SemaphoreType.DMA((ROUNDS, n)) for n in members],
        ],
        compiler_params=pltpu.CompilerParams(
            collective_id=0, has_side_effects=True, vmem_limit_bytes=56 * 1024 * 1024
        ),
    )(
        active,
        owner,
        weights,
        residual_rows,
        first_diag.reshape(1, width),
        first_rhs.reshape(1, width),
        linv,
        link,
    )
    return step.reshape(width), newton


def solution(mesh):
    shared = ("grp", "scen")
    placed = (
        P(shared, None, None),
        P(shared, None, None),
        P(shared, None),
        P(shared),
        P(shared),
        P(),
        P(),
        P(),
    )
    return jax.shard_map(
        functools.partial(body, dict(mesh.shape)),
        mesh=mesh,
        in_specs=placed,
        out_specs=(P(), P(shared, None)),
        check_vma=False,
    )
```

```python
import functools
import math

import jax
import jax.numpy as jnp
from jax import lax
from jax.experimental import pallas as pl
from jax.experimental.pallas import tpu as pltpu
from jax.sharding import PartitionSpec as P

MESH = pl.DeviceIdType.MESH
NT = (((1,), (1,)), ((), ()))
BLOCK = 256
GROUP = 2
PAD = 16
LANES = 128
ROUNDS = 3
STAGES = (("grp",), ("scen",))


def member(axes, sizes, shift):
    me = 0
    for axis in axes:
        me = me * sizes[axis] + lax.axis_index(axis)
    other = lax.rem(me + shift, math.prod(sizes[axis] for axis in axes))
    place = {}
    for axis in reversed(axes):
        place[axis] = lax.rem(other, sizes[axis])
        other = lax.div(other, sizes[axis])
    return me, place


def split(row):
    high = row.astype(jnp.bfloat16).astype(jnp.float32)
    return high, row - high


def stack(rows):
    width = rows[0].shape[1]
    numbers = lax.broadcasted_iota(jnp.int32, (PAD, width), 0)
    out = jnp.zeros((PAD, width), jnp.float32)
    for number, row in enumerate(rows):
        out = jnp.where(numbers == number, row, out)
    return out.astype(jnp.bfloat16)


def to_tile(row):
    return jnp.concatenate(
        [row[:, at : at + LANES] for at in range(0, row.shape[1], LANES)], axis=0
    )


def to_row(tile, width):
    return jnp.concatenate([tile[n : n + 1, :] for n in range(width // LANES)], axis=1)


def kernel(
    sizes,
    active_ref,
    owner_ref,
    weights_ref,
    residual_ref,
    diag_ref,
    rhs_ref,
    linv_hbm,
    link_hbm,
    step_ref,
    newton_ref,
    linv,
    link,
    lhs,
    solved,
    gram,
    back,
    *rest,
):
    count, rows, width = link.shape
    blocks = rows // BLOCK
    bufs = rest[: len(STAGES)]
    linv_sem, link_sem = rest[len(STAGES) : len(STAGES) + 2]
    send_sems = rest[len(STAGES) + 2 : 2 * len(STAGES) + 2]
    recv_sems = rest[2 * len(STAGES) + 2 :]

    def linv_copy(s, i):
        part = (s, pl.ds(i * BLOCK, BLOCK), pl.ds(0, (i + 1) * BLOCK))
        return pltpu.make_async_copy(linv_hbm.at[part], linv.at[part], linv_sem.at[s, i])

    def link_copy(s, i):
        part = (s, pl.ds(i * BLOCK, BLOCK))
        return pltpu.make_async_copy(link_hbm.at[part], link.at[part], link_sem.at[s, i])

    for s in range(count):
        for i in range(blocks):
            link_copy(s, i).start()
            linv_copy(s, i).start()

    barrier = pltpu.get_barrier_semaphore()
    partners = 0
    for axes in STAGES:
        for shift in range(1, math.prod(sizes[axis] for axis in axes)):
            pl.semaphore_signal(
                barrier, inc=1, device_id=member(axes, sizes, shift)[1], device_id_type=MESH
            )
            partners += 1

    right = residual_ref[...].astype(jnp.float32)
    for s in range(count):
        lhs[s, width:, :] = stack([right[s : s + 1, :]])

    def turn(s, i):
        columns = link[s, i * BLOCK : (i + 1) * BLOCK, :].astype(jnp.float32)
        numbers = i * BLOCK + lax.broadcasted_iota(jnp.int32, (BLOCK, width), 0)
        masked = jnp.where(numbers < active_ref[s], columns, 0.0).astype(jnp.bfloat16)
        lhs[s, :width, i * BLOCK : (i + 1) * BLOCK] = masked.T

    def solve(s, i):
        deep = (i + 1) * BLOCK
        out = lax.dot_general(
            lhs[s, :, :deep],
            linv[s, i * BLOCK : deep, :deep],
            NT,
            preferred_element_type=jnp.float32,
        )
        solved[s, :, i * BLOCK : deep] = out.astype(jnp.bfloat16)

    steps = [
        [(s, i) for i in range(at, min(at + GROUP, blocks))]
        for s in range(count)
        for at in range(0, blocks, GROUP)
    ]
    for s, i in steps[0]:
        link_copy(s, i).wait()
        turn(s, i)
    cross = jnp.zeros((1, width), jnp.float32)
    for number, step in enumerate(steps):
        later = steps[number + 1] if number + 1 < len(steps) else []
        for s, i in step:
            linv_copy(s, i).wait()
        for s, i in later:
            link_copy(s, i).wait()
        for s, i in later:
            turn(s, i)
        for s, i in step:
            solve(s, i)
        part = jnp.zeros((PAD, width), jnp.float32)
        for s, i in step:
            part = part + lax.dot_general(
                solved[s, width:, i * BLOCK : (i + 1) * BLOCK],
                solved[s, :width, i * BLOCK : (i + 1) * BLOCK],
                NT,
                preferred_element_type=jnp.float32,
            )
        cross = cross + weights_ref[owner_ref[step[0][0]]] * part[0:1, :]
    pl.semaphore_wait(barrier, partners)

    def total(turn_number, tile, beside):
        for stage, axes in enumerate(STAGES):
            buf = bufs[stage]
            n = buf.shape[1]
            me = member(axes, sizes, 0)[0]
            sent = pl.ds(0, tile.shape[0])
            buf[turn_number, me, sent] = tile
            copies = []
            for shift in range(1, n):
                copies.append(
                    pltpu.make_async_remote_copy(
                        src_ref=buf.at[turn_number, me, sent],
                        dst_ref=buf.at[turn_number, me, sent],
                        send_sem=send_sems[stage].at[turn_number, shift],
                        recv_sem=recv_sems[stage].at[turn_number, shift],
                        device_id=member(axes, sizes, shift)[1],
                        device_id_type=MESH,
                    )
                )
                copies[-1].start()
            for s in range(count):
                if s * len(STAGES) // count == stage:
                    beside(s)
            for copy in copies:
                copy.wait()
            tile = buf[turn_number, 0, sent]
            for number in range(1, n):
                tile = tile + buf[turn_number, number, sent]
        return tile

    def add_gram(s):
        part = lax.dot_general(
            solved[s, :width, :], solved[s, :width, :], NT, preferred_element_type=jnp.float32
        )
        part = weights_ref[owner_ref[s]] * part
        gram[...] = part if s == 0 else gram[...] + part

    def times_gram(row):
        part = gram[:, :LANES] * row[:, :LANES]
        for at in range(LANES, width, LANES):
            part = part + gram[:, at : at + LANES] * row[:, at : at + LANES]
        high, rest_high = split(part)
        middle, low = split(rest_high)
        parts = jnp.concatenate([high, middle, low], axis=1).astype(jnp.bfloat16)
        ones = jnp.ones((PAD, 3 * LANES), jnp.bfloat16)
        out = lax.dot_general(ones, parts, NT, preferred_element_type=jnp.float32)
        return out[0:1, :]

    def dots(left, other):
        return jnp.sum(left * other, axis=1, keepdims=True)

    diag = diag_ref[...]
    vector = rhs_ref[...] - to_row(total(0, to_tile(cross), add_gram), width)
    norm_first = dots(vector, vector)
    summed = total(1, to_tile(times_gram(vector)), lambda s: None)
    image = diag * vector + to_row(summed, width)
    alpha = norm_first / dots(vector, image)
    iterate = alpha * vector
    remain = vector - alpha * image
    norm_next = dots(remain, remain)
    direction = remain + (norm_next / norm_first) * vector
    local = dots(direction, times_gram(direction))
    both = stack([*split(iterate), *split(direction)])

    def back_solve(s):
        taken = jnp.dot(both, solved[s, :width, :], preferred_element_type=jnp.float32)
        lifted = solved[s, width:, :].astype(jnp.float32)[0:1, :]
        residue = lifted - (taken[0:1, :] + taken[1:2, :])
        slope = taken[2:3, :] + taken[3:4, :]
        sides = stack([*split(residue), *split(slope)])
        for j in range(blocks):
            back[s, :, j * BLOCK : (j + 1) * BLOCK] = jnp.dot(
                sides[:, j * BLOCK :],
                linv[s, j * BLOCK :, j * BLOCK : (j + 1) * BLOCK],
                preferred_element_type=jnp.float32,
            )

    curved = total(2, jnp.broadcast_to(local, (1, LANES)), back_solve)[0:1, 0:1]
    alpha = norm_next / (dots(direction, diag * direction) + curved)
    step_ref[...] = iterate + alpha * direction
    for s in range(count):
        newton_ref[s : s + 1, :] = (back[s, 0:1, :] + back[s, 1:2, :]) - alpha * (
            back[s, 2:3, :] + back[s, 3:4, :]
        )


def finish(step_ref, newton_ref, step_out, newton_out):
    step_out[...] = step_ref[...]
    newton_out[...] = newton_ref[...]


def body(sizes, linv, link, residual_rows, active, owner, weights, first_diag, first_rhs):
    count, rows, width = link.shape
    blocks = rows // BLOCK
    tile_rows = -(-width // (8 * LANES)) * 8
    members = [math.prod(sizes[axis] for axis in axes) for axes in STAGES]
    smem = pl.BlockSpec(memory_space=pltpu.SMEM)
    vmem = pl.BlockSpec(memory_space=pltpu.VMEM)
    hbm = pl.BlockSpec(memory_space=pl.ANY)
    shapes = (
        jax.ShapeDtypeStruct((1, width), jnp.float32),
        jax.ShapeDtypeStruct((count, rows), jnp.float32),
    )
    made = pl.pallas_call(
        functools.partial(kernel, sizes),
        out_shape=tuple(pltpu.VMEM(shape.shape, shape.dtype) for shape in shapes),
        in_specs=[smem, smem, smem, vmem, vmem, vmem, hbm, hbm],
        out_specs=(vmem, vmem),
        scratch_shapes=[
            pltpu.VMEM((count, rows, rows), jnp.bfloat16),
            pltpu.VMEM((count, rows, width), jnp.bfloat16),
            pltpu.VMEM((count, width + PAD, rows), jnp.bfloat16),
            pltpu.VMEM((count, width + PAD, rows), jnp.bfloat16),
            pltpu.VMEM((width, width), jnp.float32),
            pltpu.VMEM((count, PAD, rows), jnp.float32),
            *[pltpu.VMEM((ROUNDS, n, tile_rows, LANES), jnp.float32) for n in members],
            pltpu.SemaphoreType.DMA((count, blocks)),
            pltpu.SemaphoreType.DMA((count, blocks)),
            *[pltpu.SemaphoreType.DMA((ROUNDS, n)) for n in members],
            *[pltpu.SemaphoreType.DMA((ROUNDS, n)) for n in members],
        ],
        compiler_params=pltpu.CompilerParams(
            collective_id=0, has_side_effects=True, vmem_limit_bytes=56 * 1024 * 1024
        ),
    )(
        active,
        owner,
        weights,
        residual_rows,
        first_diag.reshape(1, width),
        first_rhs.reshape(1, width),
        linv,
        link,
    )
    step, newton = pl.pallas_call(
        finish, out_shape=shapes, in_specs=[vmem, vmem], out_specs=(vmem, vmem)
    )(*made)
    return step.reshape(width), newton


def solution(mesh):
    shared = ("grp", "scen")
    placed = (
        P(shared, None, None),
        P(shared, None, None),
        P(shared, None),
        P(shared),
        P(shared),
        P(),
        P(),
        P(),
    )
    return jax.shard_map(
        functools.partial(body, dict(mesh.shape)),
        mesh=mesh,
        in_specs=placed,
        out_specs=(P(), P(shared, None)),
        check_vma=False,
    )
```

```python
import functools
import math

import jax
import jax.numpy as jnp
from jax import lax
from jax.experimental import pallas as pl
from jax.experimental.pallas import tpu as pltpu
from jax.sharding import PartitionSpec as P

MESH = pl.DeviceIdType.MESH
NT = (((1,), (1,)), ((), ()))
BLOCK = 256
TAIL = 2
PAD = 16
LANES = 128
ROUNDS = 3
STAGES = (("grp",), ("scen",))


def member(axes, sizes, shift):
    me = 0
    for axis in axes:
        me = me * sizes[axis] + lax.axis_index(axis)
    other = lax.rem(me + shift, math.prod(sizes[axis] for axis in axes))
    place = {}
    for axis in reversed(axes):
        place[axis] = lax.rem(other, sizes[axis])
        other = lax.div(other, sizes[axis])
    return me, place


def split(row):
    high = row.astype(jnp.bfloat16).astype(jnp.float32)
    return high, row - high


def stack(rows):
    width = rows[0].shape[1]
    numbers = lax.broadcasted_iota(jnp.int32, (PAD, width), 0)
    out = jnp.zeros((PAD, width), jnp.float32)
    for number, row in enumerate(rows):
        out = jnp.where(numbers == number, row, out)
    return out.astype(jnp.bfloat16)


def to_tile(row):
    return jnp.concatenate(
        [row[:, at : at + LANES] for at in range(0, row.shape[1], LANES)], axis=0
    )


def to_row(tile, width):
    return jnp.concatenate([tile[n : n + 1, :] for n in range(width // LANES)], axis=1)


def kernel(
    sizes,
    active_ref,
    owner_ref,
    weights_ref,
    residual_ref,
    diag_ref,
    rhs_ref,
    linv_hbm,
    link_hbm,
    step_ref,
    newton_ref,
    linv,
    link,
    lhs,
    solved,
    gram,
    back,
    active,
    owner,
    weights,
    residual,
    first_diag,
    first_rhs,
    small_sem,
    *rest,
):
    count, rows, width = link.shape
    blocks = rows // BLOCK
    bufs = rest[: len(STAGES)]
    linv_sem, link_sem = rest[len(STAGES) : len(STAGES) + 2]
    send_sems = rest[len(STAGES) + 2 : 2 * len(STAGES) + 2]
    recv_sems = rest[2 * len(STAGES) + 2 :]

    def linv_copy(s, i):
        part = (s, pl.ds(i * BLOCK, BLOCK), pl.ds(0, (i + 1) * BLOCK))
        return pltpu.make_async_copy(linv_hbm.at[part], linv.at[part], linv_sem.at[s, i])

    def link_copy(s, i):
        part = (s, pl.ds(i * BLOCK, BLOCK))
        return pltpu.make_async_copy(link_hbm.at[part], link.at[part], link_sem.at[s, i])

    small = [
        pltpu.make_async_copy(source, target, small_sem.at[number])
        for number, (source, target) in enumerate(
            (
                (active_ref, active),
                (residual_ref, residual),
                (owner_ref, owner),
                (weights_ref, weights),
                (diag_ref, first_diag),
                (rhs_ref, first_rhs),
            )
        )
    ]
    for copy in small[:2]:
        copy.start()
    for s in range(count):
        for i in range(blocks):
            if s == 0 and i == 1:
                for copy in small[2:]:
                    copy.start()
            link_copy(s, i).start()
            linv_copy(s, i).start()

    barrier = pltpu.get_barrier_semaphore()
    partners = 0
    for axes in STAGES:
        for shift in range(1, math.prod(sizes[axis] for axis in axes)):
            pl.semaphore_signal(
                barrier, inc=1, device_id=member(axes, sizes, shift)[1], device_id_type=MESH
            )
            partners += 1

    for copy in small:
        copy.wait()
    right = residual[...].astype(jnp.float32)
    for s in range(count):
        lhs[s, width:, :] = stack([right[s : s + 1, :]])

    def turn(s, i):
        columns = link[s, i * BLOCK : (i + 1) * BLOCK, :].astype(jnp.float32)
        numbers = i * BLOCK + lax.broadcasted_iota(jnp.int32, (BLOCK, width), 0)
        masked = jnp.where(numbers < active[s], columns, 0.0).astype(jnp.bfloat16)
        lhs[s, :width, i * BLOCK : (i + 1) * BLOCK] = masked.T

    def solve(s, i):
        deep = (i + 1) * BLOCK
        out = lax.dot_general(
            lhs[s, :, :deep],
            linv[s, i * BLOCK : deep, :deep],
            NT,
            preferred_element_type=jnp.float32,
        )
        solved[s, :, i * BLOCK : deep] = out.astype(jnp.bfloat16)

    steps = []
    for s in range(count):
        cuts = {0, blocks, max(blocks - TAIL, 0)} if s else {0, TAIL, 2 * TAIL, blocks}
        cuts = sorted(cut for cut in cuts if cut <= blocks)
        steps += [[(s, i) for i in range(*pair)] for pair in zip(cuts, cuts[1:])]

    def crossed(step):
        s, low, high = step[0][0], step[0][1] * BLOCK, (step[-1][1] + 1) * BLOCK
        part = lax.dot_general(
            solved[s, width:, low:high],
            solved[s, :width, low:high],
            NT,
            preferred_element_type=jnp.float32,
        )
        return weights[owner[s]] * part[0:1, :]

    for s, i in steps[0]:
        link_copy(s, i).wait()
        turn(s, i)
    cross = jnp.zeros((1, width), jnp.float32)
    for number, step in enumerate(steps):
        later = steps[number + 1] if number + 1 < len(steps) else []
        for s, i in step:
            linv_copy(s, i).wait()
        for s, i in later:
            link_copy(s, i).wait()
        for s, i in later:
            turn(s, i)
        for s, i in step:
            solve(s, i)
        if number:
            cross = cross + crossed(steps[number - 1])
    cross = cross + crossed(steps[-1])
    pl.semaphore_wait(barrier, partners)

    sends = []

    def total(turn_number, tile, beside):
        for stage, axes in enumerate(STAGES):
            buf = bufs[stage]
            n = buf.shape[1]
            me = member(axes, sizes, 0)[0]
            sent = pl.ds(0, tile.shape[0])
            buf[turn_number, me, sent] = tile
            copies = []
            for shift in range(1, n):
                copies.append(
                    pltpu.make_async_remote_copy(
                        src_ref=buf.at[turn_number, me, sent],
                        dst_ref=buf.at[turn_number, me, sent],
                        send_sem=send_sems[stage].at[turn_number, shift],
                        recv_sem=recv_sems[stage].at[turn_number, shift],
                        device_id=member(axes, sizes, shift)[1],
                        device_id_type=MESH,
                    )
                )
                copies[-1].start()
            for s in range(count):
                if s * len(STAGES) // count == stage:
                    beside(s)
            for copy in copies:
                copy.wait_recv()
            sends.extend(copies)
            tile = buf[turn_number, 0, sent]
            for number in range(1, n):
                tile = tile + buf[turn_number, number, sent]
        return tile

    def add_gram(s):
        part = lax.dot_general(
            solved[s, :width, :], solved[s, :width, :], NT, preferred_element_type=jnp.float32
        )
        part = weights[owner[s]] * part
        gram[...] = part if s == 0 else gram[...] + part

    def times_gram(row):
        part = gram[:, :LANES] * row[:, :LANES]
        for at in range(LANES, width, LANES):
            part = part + gram[:, at : at + LANES] * row[:, at : at + LANES]
        high, rest_high = split(part)
        middle, low = split(rest_high)
        parts = jnp.concatenate([high, middle, low], axis=1).astype(jnp.bfloat16)
        ones = jnp.ones((PAD, 3 * LANES), jnp.bfloat16)
        out = lax.dot_general(ones, parts, NT, preferred_element_type=jnp.float32)
        return out[0:1, :]

    def dots(left, other):
        return jnp.sum(left * other, axis=1, keepdims=True)

    diag = first_diag[...]
    vector = first_rhs[...] - to_row(total(0, to_tile(cross), add_gram), width)
    norm_first = dots(vector, vector)
    summed = total(1, to_tile(times_gram(vector)), lambda s: None)
    image = diag * vector + to_row(summed, width)
    alpha = norm_first / dots(vector, image)
    iterate = alpha * vector
    remain = vector - alpha * image
    norm_next = dots(remain, remain)
    direction = remain + (norm_next / norm_first) * vector
    local = dots(direction, times_gram(direction))
    both = stack([*split(iterate), *split(direction)])

    def back_solve(s):
        taken = jnp.dot(both, solved[s, :width, :], preferred_element_type=jnp.float32)
        lifted = solved[s, width:, :].astype(jnp.float32)[0:1, :]
        residue = lifted - (taken[0:1, :] + taken[1:2, :])
        slope = taken[2:3, :] + taken[3:4, :]
        sides = stack([*split(residue), *split(slope)])
        for j in range(blocks):
            back[s, :, j * BLOCK : (j + 1) * BLOCK] = jnp.dot(
                sides[:, j * BLOCK :],
                linv[s, j * BLOCK :, j * BLOCK : (j + 1) * BLOCK],
                preferred_element_type=jnp.float32,
            )

    curved = total(2, jnp.broadcast_to(local, (1, LANES)), back_solve)[0:1, 0:1]
    alpha = norm_next / (dots(direction, diag * direction) + curved)
    step_ref[...] = iterate + alpha * direction
    for s in range(count):
        newton_ref[s : s + 1, :] = (back[s, 0:1, :] + back[s, 1:2, :]) - alpha * (
            back[s, 2:3, :] + back[s, 3:4, :]
        )
    for copy in sends:
        copy.wait_send()


def finish(step_ref, newton_ref, step_out, newton_out):
    step_out[...] = step_ref[...]
    newton_out[...] = newton_ref[...]


def body(sizes, linv, link, residual_rows, active, owner, weights, first_diag, first_rhs):
    count, rows, width = link.shape
    blocks = rows // BLOCK
    tile_rows = -(-width // (8 * LANES)) * 8
    members = [math.prod(sizes[axis] for axis in axes) for axes in STAGES]
    vmem = pl.BlockSpec(memory_space=pltpu.VMEM)
    hbm = pl.BlockSpec(memory_space=pl.ANY)
    shapes = (
        jax.ShapeDtypeStruct((1, width), jnp.float32),
        jax.ShapeDtypeStruct((count, rows), jnp.float32),
    )
    made = pl.pallas_call(
        functools.partial(kernel, sizes),
        out_shape=tuple(pltpu.VMEM(shape.shape, shape.dtype) for shape in shapes),
        in_specs=[hbm] * 8,
        out_specs=(vmem, vmem),
        scratch_shapes=[
            pltpu.VMEM((count, rows, rows), jnp.bfloat16),
            pltpu.VMEM((count, rows, width), jnp.bfloat16),
            pltpu.VMEM((count, width + PAD, rows), jnp.bfloat16),
            pltpu.VMEM((count, width + PAD, rows), jnp.bfloat16),
            pltpu.VMEM((width, width), jnp.float32),
            pltpu.VMEM((count, PAD, rows), jnp.float32),
            pltpu.SMEM(active.shape, active.dtype),
            pltpu.SMEM(owner.shape, owner.dtype),
            pltpu.SMEM(weights.shape, weights.dtype),
            pltpu.VMEM(residual_rows.shape, residual_rows.dtype),
            pltpu.VMEM((1, width), jnp.float32),
            pltpu.VMEM((1, width), jnp.float32),
            pltpu.SemaphoreType.DMA((6,)),
            *[pltpu.VMEM((ROUNDS, n, tile_rows, LANES), jnp.float32) for n in members],
            pltpu.SemaphoreType.DMA((count, blocks)),
            pltpu.SemaphoreType.DMA((count, blocks)),
            *[pltpu.SemaphoreType.DMA((ROUNDS, n)) for n in members],
            *[pltpu.SemaphoreType.DMA((ROUNDS, n)) for n in members],
        ],
        compiler_params=pltpu.CompilerParams(
            collective_id=0, has_side_effects=True, vmem_limit_bytes=56 * 1024 * 1024
        ),
    )(
        active,
        owner,
        weights,
        residual_rows,
        first_diag.reshape(1, width),
        first_rhs.reshape(1, width),
        linv,
        link,
    )
    step, newton = pl.pallas_call(
        finish,
        out_shape=shapes,
        in_specs=[vmem, vmem],
        out_specs=(vmem, vmem),
        compiler_params=pltpu.CompilerParams(vmem_limit_bytes=1024 * 1024),
    )(*made)
    return step.reshape(width), newton


def solution(mesh):
    shared = ("grp", "scen")
    placed = (
        P(shared, None, None),
        P(shared, None, None),
        P(shared, None),
        P(shared),
        P(shared),
        P(),
        P(),
        P(),
    )
    return jax.shard_map(
        functools.partial(body, dict(mesh.shape)),
        mesh=mesh,
        in_specs=placed,
        out_specs=(P(), P(shared, None)),
        check_vma=False,
    )
```

```python
import functools
import math

import jax
import jax.numpy as jnp
from jax import lax
from jax.experimental import pallas as pl
from jax.experimental.pallas import tpu as pltpu
from jax.sharding import PartitionSpec as P

MESH = pl.DeviceIdType.MESH
NT = (((1,), (1,)), ((), ()))
BLOCK = 256
TAIL = 2
PAD = 16
LANES = 128
ROUNDS = 3
STAGES = (("grp",), ("scen",))


def member(axes, sizes, shift):
    me = 0
    for axis in axes:
        me = me * sizes[axis] + lax.axis_index(axis)
    other = lax.rem(me + shift, math.prod(sizes[axis] for axis in axes))
    place = {}
    for axis in reversed(axes):
        place[axis] = lax.rem(other, sizes[axis])
        other = lax.div(other, sizes[axis])
    return me, place


def split(row):
    high = row.astype(jnp.bfloat16).astype(jnp.float32)
    return high, row - high


def stack(rows):
    width = rows[0].shape[1]
    numbers = lax.broadcasted_iota(jnp.int32, (PAD, width), 0)
    out = jnp.zeros((PAD, width), jnp.float32)
    for number, row in enumerate(rows):
        out = jnp.where(numbers == number, row, out)
    return out.astype(jnp.bfloat16)


def to_tile(row):
    return jnp.concatenate(
        [row[:, at : at + LANES] for at in range(0, row.shape[1], LANES)], axis=0
    )


def to_row(tile, width):
    return jnp.concatenate([tile[n : n + 1, :] for n in range(width // LANES)], axis=1)


def kernel(
    sizes,
    active_ref,
    owner_ref,
    weights_ref,
    residual_ref,
    diag_ref,
    rhs_ref,
    linv_hbm,
    link_hbm,
    step_ref,
    newton_ref,
    linv,
    link,
    lhs,
    solved,
    gram,
    back,
    active,
    owner,
    weights,
    residual,
    first_diag,
    first_rhs,
    small_sem,
    *rest,
):
    count, rows, width = link.shape
    blocks = rows // BLOCK
    bufs = rest[: len(STAGES)]
    linv_sem, link_sem = rest[len(STAGES) : len(STAGES) + 2]
    send_sems = rest[len(STAGES) + 2 : 2 * len(STAGES) + 2]
    recv_sems = rest[2 * len(STAGES) + 2 :]

    def linv_copy(s, i):
        part = (s, pl.ds(i * BLOCK, BLOCK), pl.ds(0, (i + 1) * BLOCK))
        return pltpu.make_async_copy(linv_hbm.at[part], linv.at[part], linv_sem.at[s, i])

    def link_copy(s, i):
        part = (s, pl.ds(i * BLOCK, BLOCK))
        return pltpu.make_async_copy(link_hbm.at[part], link.at[part], link_sem.at[s, i])

    small = [
        pltpu.make_async_copy(source, target, small_sem.at[number])
        for number, (source, target) in enumerate(
            (
                (active_ref, active),
                (residual_ref, residual),
                (owner_ref, owner),
                (weights_ref, weights),
                (diag_ref, first_diag),
                (rhs_ref, first_rhs),
            )
        )
    ]
    for copy in small[:2]:
        copy.start()
    for s in range(count):
        for i in range(blocks):
            if s == 0 and i == 1:
                for copy in small[2:]:
                    copy.start()
            link_copy(s, i).start()
            linv_copy(s, i).start()

    barrier = pltpu.get_barrier_semaphore()
    partners = 0
    for axes in STAGES:
        for shift in range(1, math.prod(sizes[axis] for axis in axes)):
            pl.semaphore_signal(
                barrier, inc=1, device_id=member(axes, sizes, shift)[1], device_id_type=MESH
            )
            partners += 1

    for copy in small:
        copy.wait()
    right = residual[...].astype(jnp.float32)
    for s in range(count):
        lhs[s, width:, :] = stack([right[s : s + 1, :]])

    def turn(s, i):
        columns = link[s, i * BLOCK : (i + 1) * BLOCK, :].astype(jnp.float32)
        numbers = i * BLOCK + lax.broadcasted_iota(jnp.int32, (BLOCK, width), 0)
        masked = jnp.where(numbers < active[s], columns, 0.0).astype(jnp.bfloat16)
        lhs[s, :width, i * BLOCK : (i + 1) * BLOCK] = masked.T

    def solve(s, i):
        deep = (i + 1) * BLOCK
        out = lax.dot_general(
            lhs[s, :, :deep],
            linv[s, i * BLOCK : deep, :deep],
            NT,
            preferred_element_type=jnp.float32,
        )
        solved[s, :, i * BLOCK : deep] = out.astype(jnp.bfloat16)

    steps = []
    for s in range(count):
        cuts = {0, blocks, max(blocks - TAIL, 0)} if s else {0, TAIL, 2 * TAIL, blocks}
        cuts = sorted(cut for cut in cuts if cut <= blocks)
        steps += [[(s, i) for i in range(*pair)] for pair in zip(cuts, cuts[1:])]

    def crossed(step):
        s, low, high = step[0][0], step[0][1] * BLOCK, (step[-1][1] + 1) * BLOCK
        part = lax.dot_general(
            solved[s, width:, low:high],
            solved[s, :width, low:high],
            NT,
            preferred_element_type=jnp.float32,
        )
        return weights[owner[s]] * part[0:1, :]

    for s, i in steps[0]:
        link_copy(s, i).wait()
        turn(s, i)
    cross = jnp.zeros((1, width), jnp.float32)
    for number, step in enumerate(steps):
        later = steps[number + 1] if number + 1 < len(steps) else []
        for s, i in step:
            linv_copy(s, i).wait()
        for s, i in later:
            link_copy(s, i).wait()
        for s, i in later:
            turn(s, i)
        for s, i in step:
            solve(s, i)
        if number:
            cross = cross + crossed(steps[number - 1])
    cross = cross + crossed(steps[-1])
    pl.semaphore_wait(barrier, partners)

    sends = []

    def total(turn_number, tile, beside):
        for stage, axes in enumerate(STAGES):
            buf = bufs[stage]
            n = buf.shape[1]
            me = member(axes, sizes, 0)[0]
            sent = pl.ds(0, tile.shape[0])
            buf[turn_number, me, sent] = tile
            copies = []
            for shift in range(1, n):
                copies.append(
                    pltpu.make_async_remote_copy(
                        src_ref=buf.at[turn_number, me, sent],
                        dst_ref=buf.at[turn_number, me, sent],
                        send_sem=send_sems[stage].at[turn_number, shift],
                        recv_sem=recv_sems[stage].at[turn_number, shift],
                        device_id=member(axes, sizes, shift)[1],
                        device_id_type=MESH,
                    )
                )
                copies[-1].start()
            for s in range(count):
                if s * len(STAGES) // count == stage:
                    beside(s)
            for copy in copies:
                copy.wait_recv()
            sends.extend(copies)
            tile = buf[turn_number, 0, sent]
            for number in range(1, n):
                tile = tile + buf[turn_number, number, sent]
        return tile

    def add_gram(s):
        half = width // 2
        for low, high in ((0, half), (half, width)):
            part = lax.dot_general(
                solved[s, low:high, :],
                solved[s, low:width, :],
                NT,
                preferred_element_type=jnp.float32,
            )
            part = weights[owner[s]] * part
            gram[low:high, low:] = part if s == 0 else gram[low:high, low:] + part
        if s == count - 1:
            gram[half:, :half] = gram[:half, half:].T

    def times_gram(row):
        part = gram[:, :LANES] * row[:, :LANES]
        for at in range(LANES, width, LANES):
            part = part + gram[:, at : at + LANES] * row[:, at : at + LANES]
        high, rest_high = split(part)
        middle, low = split(rest_high)
        parts = jnp.concatenate([high, middle, low], axis=1).astype(jnp.bfloat16)
        ones = jnp.ones((PAD, 3 * LANES), jnp.bfloat16)
        out = lax.dot_general(ones, parts, NT, preferred_element_type=jnp.float32)
        return out[0:1, :]

    def dots(left, other):
        return jnp.sum(left * other, axis=1, keepdims=True)

    diag = first_diag[...]
    vector = first_rhs[...] - to_row(total(0, to_tile(cross), add_gram), width)
    norm_first = dots(vector, vector)
    summed = total(1, to_tile(times_gram(vector)), lambda s: None)
    image = diag * vector + to_row(summed, width)
    alpha = norm_first / dots(vector, image)
    iterate = alpha * vector
    remain = vector - alpha * image
    norm_next = dots(remain, remain)
    direction = remain + (norm_next / norm_first) * vector
    local = dots(direction, times_gram(direction))
    both = stack([*split(iterate), *split(direction)])

    def back_solve(s):
        taken = jnp.dot(both, solved[s, :width, :], preferred_element_type=jnp.float32)
        lifted = solved[s, width:, :].astype(jnp.float32)[0:1, :]
        residue = lifted - (taken[0:1, :] + taken[1:2, :])
        slope = taken[2:3, :] + taken[3:4, :]
        sides = stack([*split(residue), *split(slope)])
        for j in range(blocks):
            back[s, :, j * BLOCK : (j + 1) * BLOCK] = jnp.dot(
                sides[:, j * BLOCK :],
                linv[s, j * BLOCK :, j * BLOCK : (j + 1) * BLOCK],
                preferred_element_type=jnp.float32,
            )

    curved = total(2, jnp.broadcast_to(local, (1, LANES)), back_solve)[0:1, 0:1]
    alpha = norm_next / (dots(direction, diag * direction) + curved)
    step_ref[...] = iterate + alpha * direction
    for s in range(count):
        newton_ref[s : s + 1, :] = (back[s, 0:1, :] + back[s, 1:2, :]) - alpha * (
            back[s, 2:3, :] + back[s, 3:4, :]
        )
    for copy in sends:
        copy.wait_send()


def finish(step_ref, newton_ref, step_out, newton_out):
    step_out[...] = step_ref[...]
    newton_out[...] = newton_ref[...]


def body(sizes, linv, link, residual_rows, active, owner, weights, first_diag, first_rhs):
    count, rows, width = link.shape
    blocks = rows // BLOCK
    tile_rows = -(-width // (8 * LANES)) * 8
    members = [math.prod(sizes[axis] for axis in axes) for axes in STAGES]
    vmem = pl.BlockSpec(memory_space=pltpu.VMEM)
    hbm = pl.BlockSpec(memory_space=pl.ANY)
    shapes = (
        jax.ShapeDtypeStruct((1, width), jnp.float32),
        jax.ShapeDtypeStruct((count, rows), jnp.float32),
    )
    made = pl.pallas_call(
        functools.partial(kernel, sizes),
        out_shape=tuple(pltpu.VMEM(shape.shape, shape.dtype) for shape in shapes),
        in_specs=[hbm] * 8,
        out_specs=(vmem, vmem),
        scratch_shapes=[
            pltpu.VMEM((count, rows, rows), jnp.bfloat16),
            pltpu.VMEM((count, rows, width), jnp.bfloat16),
            pltpu.VMEM((count, width + PAD, rows), jnp.bfloat16),
            pltpu.VMEM((count, width + PAD, rows), jnp.bfloat16),
            pltpu.VMEM((width, width), jnp.float32),
            pltpu.VMEM((count, PAD, rows), jnp.float32),
            pltpu.SMEM(active.shape, active.dtype),
            pltpu.SMEM(owner.shape, owner.dtype),
            pltpu.SMEM(weights.shape, weights.dtype),
            pltpu.VMEM(residual_rows.shape, residual_rows.dtype),
            pltpu.VMEM((1, width), jnp.float32),
            pltpu.VMEM((1, width), jnp.float32),
            pltpu.SemaphoreType.DMA((6,)),
            *[pltpu.VMEM((ROUNDS, n, tile_rows, LANES), jnp.float32) for n in members],
            pltpu.SemaphoreType.DMA((count, blocks)),
            pltpu.SemaphoreType.DMA((count, blocks)),
            *[pltpu.SemaphoreType.DMA((ROUNDS, n)) for n in members],
            *[pltpu.SemaphoreType.DMA((ROUNDS, n)) for n in members],
        ],
        compiler_params=pltpu.CompilerParams(
            collective_id=0, has_side_effects=True, vmem_limit_bytes=56 * 1024 * 1024
        ),
    )(
        active,
        owner,
        weights,
        residual_rows,
        first_diag.reshape(1, width),
        first_rhs.reshape(1, width),
        linv,
        link,
    )
    step, newton = pl.pallas_call(
        finish,
        out_shape=shapes,
        in_specs=[vmem, vmem],
        out_specs=(vmem, vmem),
        compiler_params=pltpu.CompilerParams(vmem_limit_bytes=1024 * 1024),
    )(*made)
    return step.reshape(width), newton


def solution(mesh):
    shared = ("grp", "scen")
    placed = (
        P(shared, None, None),
        P(shared, None, None),
        P(shared, None),
        P(shared),
        P(shared),
        P(),
        P(),
        P(),
    )
    return jax.shard_map(
        functools.partial(body, dict(mesh.shape)),
        mesh=mesh,
        in_specs=placed,
        out_specs=(P(), P(shared, None)),
        check_vma=False,
    )
```
